256 devices in a mesh: layer: 64 (over x, z, core), col: 4 (over y).
Axes of the slice: x: 4, y: 4, z: 8, core: 2. Of those that a mesh axis runs over, the one named last changes fastest.
Arguments:
- l_panels: bfloat16 [64, 2048, 2048], P('layer', None, 'col'), may hold values from -6 to 6
- u_panels: bfloat16 [64, 2048, 2048], P('layer', None, 'col'), may hold values from -0.125 to 0.125
- l_masks: int32 [64, 8, 8], P('layer'), may hold values 0 or 1
- u_masks: int32 [64, 8, 8], P('layer'), may hold values 0 or 1
- ancestor_tiles: int32 [8, 8], replicated, may hold values 0 or 1
- initial: float32 [2048, 2048], P('layer', 'col'), may hold values from -6 to 6
Outputs:
- schur: float32 [2048, 2048], P('layer', 'col')
The draws below stay inside these ranges and needn't reach their ends.
All inputs are finite; a program needn't handle non-finite values. No bound on the sum of `l_masks` or of `u_masks` on one device may be relied on, other than what follows from the above.
Results may differ from the reference program's by a relative error of at most 0.0003.
Values may be sent and summed in bfloat16 or wider, within the bound.
A program may use at most 64 MiB of HBM per device.

```python
import jax
import jax.numpy as jnp
from jax import lax

M = 2048
KD = 2048
TILE = 256
MT = 8
KT = 8
LAYERS = 64


def with_ends(array, stream_key, least, largest):
    longest = array.shape.index(max(array.shape))
    spots = []
    for shift in (0, 1):
        where = [jax.random.randint(jax.random.fold_in(stream_key, axis), (), 0, length) for axis, length in enumerate(array.shape)]
        where[longest] = (where[longest] + shift) % array.shape[longest]
        spots.append(tuple(where))
    return array.at[spots[0]].set(least).at[spots[1]].set(largest)


def shard_levels(rng, dims, shards, smallest, high):
    gain, own = 1.0, jax.random.fold_in(rng, 6)
    for dim, parts in shards:
        steps = jnp.exp(jax.random.uniform(jax.random.fold_in(own, dim), (parts,), jnp.float32, smallest / len(shards), high / len(shards)))
        gain = gain * jnp.repeat(steps, dims[dim] // parts).reshape([-1 if axis == dim else 1 for axis in range(len(dims))])
    return gain


def noise(own_key, shape, spread, reach, split=(), dtype=jnp.bfloat16):
    entries = spread * jax.random.normal(own_key, shape, jnp.float32)
    if split:
        entries = entries * shard_levels(own_key, shape, split, -0.22, 0.18)
    return jnp.clip(entries, -reach, reach).astype(dtype)


def setup_inputs(seed: int = 0) -> dict:
    key_of = jax.random.split(jax.random.key(seed), 7)
    return {
        "l_panels": noise(key_of[0], (LAYERS, M, KD), 1.0, 6.0, ((0, 64), (2, 4))),
        "u_panels": noise(key_of[1], (LAYERS, KD, M), KD ** -0.5, 0.125, ((0, 64), (2, 4))),
        "l_masks": with_ends((jax.random.randint(key_of[2], (LAYERS, MT, KT), 0, 2) < 1).astype(jnp.int32), jax.random.fold_in(key_of[2], 1), 0, 1),
        "u_masks": with_ends((jax.random.randint(key_of[3], (LAYERS, KT, MT), 0, 2) < 1).astype(jnp.int32), jax.random.fold_in(key_of[3], 1), 0, 1),
        "ancestor_tiles": with_ends((jax.random.randint(key_of[4], (MT, MT), 0, 4) < 3).astype(jnp.int32), jax.random.fold_in(key_of[4], 1), 0, 1),
        "initial": noise(key_of[5], (M, M), 1.0, 6.0, ((0, 64), (1, 4)), jnp.float32),
    }


def expand_tiles(mask):
    return jnp.repeat(jnp.repeat(mask, TILE, 0), TILE, 1)


def reference(l_panels, u_panels, l_masks, u_masks, ancestor_tiles, initial):
    def one_layer(total, items):
        lpanel, upanel, lmask, umask = items
        lpart = lpanel * expand_tiles(lmask).astype(jnp.bfloat16)
        upart = upanel * expand_tiles(umask).astype(jnp.bfloat16)
        return total + jnp.dot(lpart, upart, preferred_element_type=jnp.float32), None

    total, _ = lax.scan(one_layer, jnp.zeros((M, M), jnp.float32), (l_panels, u_panels, l_masks, u_masks))
    return initial - expand_tiles(ancestor_tiles).astype(jnp.float32) * total
```

```python
import jax
import jax.numpy as jnp
from jax import lax
from jax.experimental import pallas as pl
from jax.experimental.pallas import tpu as pltpu
from jax.sharding import PartitionSpec as P

MESH = pl.DeviceIdType.MESH
TILE = 256
NX, NY, NZ = 4, 4, 8
DEPTH = 512
PIECE = 256
CHUNK = 64
CODES = 16
LEVELS = 32000.0
STEPS = 8.0


def encode(block, codes, where):
    rows, cols = block.shape
    top = jnp.maximum(jnp.max(jnp.abs(block), axis=0, keepdims=True), 2.0**-100)
    level = jnp.ceil(jnp.log2(top) * STEPS) + 1.0
    factor = jnp.exp2(level * (-1.0 / STEPS)) * LEVELS
    codes[(*where, pl.ds(0, rows), slice(None))] = jnp.round(block * factor).astype(jnp.int32).astype(jnp.int16)
    codes[(*where, pl.ds(rows, CODES), slice(None))] = (
        jnp.broadcast_to(level, (CODES, cols)).astype(jnp.int32).astype(jnp.int16)
    )


def decode(codes, where, rows):
    level = codes[(*where, pl.ds(rows, CODES), slice(None))].astype(jnp.int32).astype(jnp.float32)[0:1]
    factor = jnp.exp2(level * (1.0 / STEPS)) * (1.0 / LEVELS)
    return codes[(*where, pl.ds(0, rows), slice(None))].astype(jnp.int32).astype(jnp.float32) * factor


def kernel(
    l_hbm, u_hbm, lmask, umask, ancestor, initial, out,
    lbuf, uown, ubuf, part, x1s, x1r, x2s, x2r, ssum, zs, zr, ys, yr, total, cs, cr,
    in_sem, a_send, a_recv, l_send, l_recv, x1_send, x1_recv, x2_send, x2_recv,
    z_send, z_recv, y_send, y_recv, c_send, c_recv,
):
    layer = lax.axis_index("layer")
    y = lax.axis_index("col")
    x = layer // (2 * NZ)
    z = (layer // 2) % NZ
    core = layer % 2
    xa = x + 1 - 2 * (x % 2)
    xb = 3 - x
    xd = 3 - xa

    def at(x_, y_, z_, c_):
        return ((x_ * NZ + z_) * 2 + c_, y_)

    def ydev(step, k):
        return at(x, (y + step) % NY, z, (core + k) % 2)

    sibling = at(x, y, z, 1 - core)
    partners = [sibling]
    partners += [ydev(step, k) for step in (1, 2, 3) for k in (0, 1)]
    partners += [at(xa, y, z, core), at(xb, y, z, core)]
    partners += [at(x, y, (z + i) % NZ, core) for i in range(1, NZ)]
    partners += [at(x, (y + 2) % NY, (z + i) % NZ, core) for i in range(1, NZ)]

    def rows_of(first, count):
        return pl.ds(pl.multiple_of(first, count), count)

    u_order = [(y + step) % NY for step in (1, 3, 2, 0)]
    l_order = [xd, xa, xb, x]
    u_in = [
        pltpu.make_async_copy(u_hbm.at[0, rows_of(b * DEPTH, DEPTH)], uown.at[rows_of(b * DEPTH, DEPTH)], in_sem.at[n])
        for n, b in enumerate(u_order)
    ]
    l_in = [
        pltpu.make_async_copy(l_hbm.at[0, rows_of(b * DEPTH, DEPTH)], lbuf.at[0, rows_of(b * DEPTH, DEPTH)], in_sem.at[4 + n])
        for n, b in enumerate(l_order)
    ]
    for n in range(4):
        u_in[n].start()
        l_in[n].start()
    barrier = pltpu.get_barrier_semaphore()
    for partner in partners:
        pl.semaphore_signal(barrier, inc=1, device_id=partner, device_id_type=MESH)

    def mask_u(block):
        for t in range(2):
            rows = rows_of(block * DEPTH + t * TILE, TILE)
            for h in range(2):
                keep = umask[0, block * 2 + t, y * 2 + h].astype(jnp.float32)
                cols = pl.ds(h * TILE, TILE)
                uown[rows, cols] = uown[rows, cols] * jnp.full((TILE, TILE), keep).astype(jnp.bfloat16)

    def mask_l(block):
        for t in range(2):
            rows = rows_of(block * DEPTH + t * TILE, TILE)
            for h in range(2):
                keep = lmask[0, block * 2 + t, y * 2 + h].astype(jnp.float32)
                cols = pl.ds(h * TILE, TILE)
                lbuf[0, rows, cols] = lbuf[0, rows, cols] * jnp.full((TILE, TILE), keep).astype(jnp.bfloat16)

    def send_u(step, k):
        block = (y + step) % NY
        to = (core + k) % 2
        slot = (NY - step) % NY
        src = uown.at[rows_of(block * DEPTH, DEPTH), pl.ds(pl.multiple_of(to * TILE, TILE), TILE)]
        return pltpu.make_async_remote_copy(
            src, ubuf.at[slot, k], a_send.at[slot * 2 + k], a_recv.at[slot * 2 + k],
            device_id=ydev(step, k), device_id_type=MESH,
        )

    def send_l(n):
        rows = rows_of(l_order[n] * DEPTH, DEPTH)
        return pltpu.make_async_remote_copy(
            lbuf.at[0, rows], lbuf.at[1, rows], l_send.at[n], l_recv.at[n], device_id=sibling, device_id_type=MESH,
        )

    u_in[0].wait()
    mask_u(u_order[0])
    u_in[1].wait()
    mask_u(u_order[1])
    pl.semaphore_wait(barrier, len(partners))
    for step in (1, 3):
        for k in range(2):
            send_u(step, k).start()
    u_in[3].wait()
    mask_u(u_order[3])
    send_u(0, 1).start()
    for n in range(4):
        l_in[n].wait()
        mask_l(l_order[n])
        send_l(n).start()
    u_in[2].wait()
    mask_u(u_order[2])
    for k in range(2):
        send_u(2, k).start()
    own = uown[rows_of(y * DEPTH, DEPTH), pl.ds(pl.multiple_of(core * TILE, TILE), TILE)]
    ubuf[0, 0] = own

    def product(s, first):
        rows = rows_of(first, PIECE)
        return jnp.dot(lbuf[0, rows], ubuf[s, 0], preferred_element_type=jnp.float32) + jnp.dot(
            lbuf[1, rows], ubuf[s, 1], preferred_element_type=jnp.float32
        )

    def x1_copy(s, q):
        return pltpu.make_async_remote_copy(
            x1s.at[s, q], x1r.at[s, q], x1_send.at[s * 2 + q], x1_recv.at[s * 2 + q],
            device_id=at(xb if q else xa, y, z, core), device_id_type=MESH,
        )

    def x2_copy(s, q):
        return pltpu.make_async_remote_copy(
            x2s.at[s, q], x2r.at[s, q], x2_send.at[s * 2 + q], x2_recv.at[s * 2 + q],
            device_id=at(xa if q else xb, y, z, core), device_id_type=MESH,
        )

    def z_copy(s, i):
        return pltpu.make_async_remote_copy(
            zs.at[s, i], zr.at[s, i], z_send.at[s * NZ + i], z_recv.at[s * NZ + i],
            device_id=at(x, (y + 2) % NY if s == 2 else y, (z + i) % NZ, core), device_id_type=MESH,
        )

    def y_copy(n):
        return pltpu.make_async_remote_copy(
            ys.at[n], yr.at[n], y_send.at[n], y_recv.at[n], device_id=ydev((1, 3)[n], 0), device_id_type=MESH,
        )

    def multiply(s):
        for q in range(2):
            for i in range(2):
                goal = xd if i else (xb if q else xa)
                encode(product(s, goal * 2 * PIECE + q * PIECE), x1s, (s, q, i))
            x1_copy(s, q).start()
        for q in range(2):
            for i in range(2):
                goal = ((xa if q else xb) if i else x)
                part[s, q, i] = product(s, goal * 2 * PIECE + q * PIECE)

    def after_x1(s):
        for q in range(2):
            x1_copy(s, q).wait_recv()
            encode(part[s, q, 1] + decode(x1r, (s, q, 1), PIECE), x2s, (s, q))
            x2_copy(s, q).start()
        for q in range(2):
            part[s, q, 0] = part[s, q, 0] + decode(x1r, (s, q, 0), PIECE)

    hops = {2: (4, 3, 5, 2, 6, 1, 7, 0)}

    def after_x2(s):
        for q in range(2):
            x2_copy(s, q).wait_recv()
            ssum[s, pl.ds(q * PIECE, PIECE)] = part[s, q, 0] + decode(x2r, (s, q), PIECE)
        for i in hops.get(s, (4, 3, 5, 2, 6, 1, 7)):
            encode(ssum[s, rows_of((z + i) % NZ * CHUNK, CHUNK)], zs, (s, i))
            z_copy(s, i).start()

    def after_z(s):
        result = None if s == 2 else ssum[s, rows_of(z * CHUNK, CHUNK)]
        for i in (1, 7, 2, 6, 3, 5, 4, 0) if s == 2 else (1, 7, 2, 6, 3, 5, 4):
            z_copy(s, i).wait_recv()
            piece = decode(zr, (s, i), CHUNK)
            result = piece if result is None else result + piece
        return result

    def arrived(s):
        for k in range(2):
            send_u((NY - s) % NY, k).wait_recv()

    send_u(0, 1).wait_recv()
    for n in range(4):
        send_l(n).wait_recv()
    multiply(0)
    after_x1(0)
    arrived(1)
    multiply(1)
    arrived(3)
    multiply(3)
    after_x2(0)
    after_x1(1)
    after_x1(3)
    arrived(2)
    multiply(2)
    total[...] = after_z(0)
    after_x2(1)
    after_x2(3)
    after_x1(2)
    ys[0] = after_z(1)
    y_copy(0).start()
    ys[1] = after_z(3)
    y_copy(1).start()
    after_x2(2)
    for n in range(2):
        y_copy(n).wait_recv()
    total[...] = total[...] + yr[0] + yr[1] + after_z(2)
    half = CHUNK // 2
    cs[...] = total[rows_of((1 - core) * half, half)]
    across = pltpu.make_async_remote_copy(cs, cr, c_send.at[0], c_recv.at[0], device_id=sibling, device_id_type=MESH)
    across.start()

    def finish(side, value):
        keep = ancestor[layer // (TILE // half), y * 2 + side].astype(jnp.float32)
        cols = pl.ds(pl.multiple_of(side * TILE, TILE), TILE)
        out[:, cols] = initial[:, cols] - keep * value

    finish(core, total[rows_of(core * half, half)])
    across.wait_recv()
    finish(1 - core, cr[...])

    for step in (1, 3, 2):
        for k in range(2):
            send_u(step, k).wait_send()
    send_u(0, 1).wait_send()
    for n in range(4):
        send_l(n).wait_send()
    for s in range(4):
        for q in range(2):
            x1_copy(s, q).wait_send()
            x2_copy(s, q).wait_send()
        for i in range(0 if s == 2 else 1, NZ):
            z_copy(s, i).wait_send()
    for n in range(2):
        y_copy(n).wait_send()
    across.wait_send()


def local(l_panels, u_panels, l_masks, u_masks, ancestor_tiles, initial):
    any_spec = pl.BlockSpec(memory_space=pl.ANY)
    smem = pl.BlockSpec(memory_space=pltpu.SMEM)
    vmem = pl.BlockSpec(memory_space=pltpu.VMEM)
    dma = pltpu.SemaphoreType.DMA
    bf16, f32, i16 = jnp.bfloat16, jnp.float32, jnp.int16
    return pl.pallas_call(
        kernel,
        out_shape=jax.ShapeDtypeStruct(initial.shape, f32),
        in_specs=[any_spec, any_spec, smem, smem, smem, vmem],
        out_specs=vmem,
        scratch_shapes=[
            pltpu.VMEM((2, 2048, DEPTH), bf16),
            pltpu.VMEM((2048, DEPTH), bf16),
            pltpu.VMEM((NY, 2, DEPTH, TILE), bf16),
            pltpu.VMEM((NY, 2, 2, PIECE, TILE), f32),
            pltpu.VMEM((NY, 2, 2, PIECE + CODES, TILE), i16),
            pltpu.VMEM((NY, 2, 2, PIECE + CODES, TILE), i16),
            pltpu.VMEM((NY, 2, PIECE + CODES, TILE), i16),
            pltpu.VMEM((NY, 2, PIECE + CODES, TILE), i16),
            pltpu.VMEM((NY, 2 * PIECE, TILE), f32),
            pltpu.VMEM((NY, NZ, CHUNK + CODES, TILE), i16),
            pltpu.VMEM((NY, NZ, CHUNK + CODES, TILE), i16),
            pltpu.VMEM((2, CHUNK, TILE), f32),
            pltpu.VMEM((2, CHUNK, TILE), f32),
            pltpu.VMEM((CHUNK, TILE), f32),
            pltpu.VMEM((CHUNK // 2, TILE), f32),
            pltpu.VMEM((CHUNK // 2, TILE), f32),
            dma((8,)),
            dma((8,)), dma((8,)),
            dma((4,)), dma((4,)),
            dma((8,)), dma((8,)),
            dma((8,)), dma((8,)),
            dma((NY * NZ,)), dma((NY * NZ,)),
            dma((2,)), dma((2,)),
            dma((1,)), dma((1,)),
        ],
        compiler_params=pltpu.CompilerParams(
            collective_id=0, has_side_effects=True, vmem_limit_bytes=56 * 2**20
        ),
    )(l_panels, u_panels, l_masks, u_masks, ancestor_tiles, initial)


def solution(mesh):
    return jax.shard_map(
        local,
        mesh=mesh,
        in_specs=(
            P("layer", None, "col"),
            P("layer", None, "col"),
            P("layer", None, None),
            P("layer", None, None),
            P(),
            P("layer", "col"),
        ),
        out_specs=P("layer", "col"),
        check_vma=False,
    )
```

```python
import jax
import jax.numpy as jnp
from jax import lax
from jax.experimental import pallas as pl
from jax.experimental.pallas import tpu as pltpu
from jax.sharding import PartitionSpec as P

MESH = pl.DeviceIdType.MESH
TILE = 256
NX, NY, NZ = 4, 4, 8
DEPTH = 512
PIECE = 256
CHUNK = 64
CODES = 16
COLS = 128
LEVELS = 32000.0
STEPS = 8.0


def encode(block, codes, where):
    rows, cols = block.shape
    top = jnp.maximum(jnp.max(jnp.abs(block), axis=0, keepdims=True), 2.0**-100)
    level = jnp.ceil(jnp.log2(top) * STEPS) + 1.0
    factor = jnp.exp2(level * (-1.0 / STEPS)) * LEVELS
    codes[(*where, pl.ds(0, rows), slice(None))] = jnp.round(block * factor).astype(jnp.int32).astype(jnp.int16)
    codes[(*where, pl.ds(rows, CODES), slice(None))] = (
        jnp.broadcast_to(level, (CODES, cols)).astype(jnp.int32).astype(jnp.int16)
    )


def decode(codes, where, rows):
    level = codes[(*where, pl.ds(rows, CODES), slice(None))].astype(jnp.int32).astype(jnp.float32)[0:1]
    factor = jnp.exp2(level * (1.0 / STEPS)) * (1.0 / LEVELS)
    return codes[(*where, pl.ds(0, rows), slice(None))].astype(jnp.int32).astype(jnp.float32) * factor


UNITS = ((0, 0), (0, 1), (1, 0), (1, 1), (3, 0), (3, 1), (2, 0), (2, 1))
TYPES = "ABAABBAA"
ORDER = (
    ("u", 0), ("u", 1), ("x1", 0), ("u", 2), ("u", 4), ("h", 1),
    ("x2", 0), ("x1", 2), ("u", 3), ("u", 5), ("x1", 1), ("h", 4),
    ("x2", 2), ("x1", 3), ("u", 6), ("x2", 1), ("z", 0), ("x1", 4),
    ("h", 5), ("x2", 3), ("x1", 6), ("u", 7), ("z", 2), ("x2", 4),
    ("x1", 5), ("z", 1), ("x2", 6), ("x1", 7), ("z", 3), ("z", 4),
    ("x2", 5), ("x2", 7), ("z", 6), ("z", 5), ("z", 7),
)
SPLIT = tuple(n for n, kind in enumerate(TYPES) if kind == "B")


def kernel(
    l_hbm, u_hbm, lmask, umask, ancestor, initial, out,
    lbuf, uown, ubuf, stage, hs, hr, part, x1s, x1r, x2s, x2r, ssum, zs, zr, ys, yr, total, cs, cr,
    in_sem, a_send, a_recv, l_send, l_recv, h_send, h_recv, x1_send, x1_recv, x2_send, x2_recv,
    z_send, z_recv, y_send, y_recv, c_send, c_recv,
):
    layer = lax.axis_index("layer")
    y = lax.axis_index("col")
    x = layer // (2 * NZ)
    z = (layer // 2) % NZ
    core = layer % 2
    xa = x + 1 - 2 * (x % 2)
    xb = 3 - x
    xd = 3 - xa
    odd = z % 2
    za = z + 1 - 2 * odd
    zb = (z + 2 * odd + NZ - 1) % NZ

    def at(x_, y_, z_, c_):
        return ((x_ * NZ + z_) * 2 + c_, y_)

    def ydev(step, k):
        return at(x, (y + step) % NY, z, (core + k) % 2)

    sibling = at(x, y, z, 1 - core)
    partners = [sibling]
    partners += [ydev(step, k) for step in (1, 2, 3) for k in (0, 1)]
    partners += [at(xa, y, z, core), at(xb, y, z, core)]
    partners += [at(x, y, (z + i) % NZ, core) for i in range(1, NZ)]
    partners += [at(x, (y + 2) % NY, (z + i) % NZ, core) for i in range(1, NZ)]

    def rows_of(first, count):
        return pl.ds(pl.multiple_of(first, count), count)

    u_order = [(y + step) % NY for step in (1, 3, 2, 0)]
    l_order = [xd, xa, xb, x]
    u_in = [
        pltpu.make_async_copy(u_hbm.at[0, rows_of(b * DEPTH, DEPTH)], uown.at[rows_of(b * DEPTH, DEPTH)], in_sem.at[n])
        for n, b in enumerate(u_order)
    ]
    l_in = [
        pltpu.make_async_copy(l_hbm.at[0, rows_of(b * DEPTH, DEPTH)], lbuf.at[0, rows_of(b * DEPTH, DEPTH)], in_sem.at[4 + n])
        for n, b in enumerate(l_order)
    ]
    for n in (0, 1, 3):
        u_in[n].start()
    for n in range(4):
        l_in[n].start()
    u_in[2].start()
    barrier = pltpu.get_barrier_semaphore()
    for partner in partners:
        pl.semaphore_signal(barrier, inc=1, device_id=partner, device_id_type=MESH)

    def mask_tiles(ref, where, mask, block):
        for t in range(2):
            rows = rows_of(block * DEPTH + t * TILE, TILE)
            for h in range(2):
                keep = mask[0, block * 2 + t, y * 2 + h].astype(jnp.float32)
                spot = (*where, rows, pl.ds(h * TILE, TILE))
                ref[spot] = ref[spot] * jnp.full((TILE, TILE), keep).astype(jnp.bfloat16)

    def number(s, h):
        return UNITS.index((s, h))

    def send_u(step, k, h):
        n = number((NY - step) % NY, h)
        cols = pl.ds(pl.multiple_of((core + k) % 2 * TILE + h * COLS, COLS), COLS)
        return pltpu.make_async_remote_copy(
            uown.at[rows_of((y + step) % NY * DEPTH, DEPTH), cols], ubuf.at[n, k],
            a_send.at[n * 2 + k], a_recv.at[n * 2 + k], device_id=ydev(step, k), device_id_type=MESH,
        )

    def send_l(n):
        rows = rows_of(l_order[n] * DEPTH, DEPTH)
        return pltpu.make_async_remote_copy(
            lbuf.at[0, rows], lbuf.at[1, rows], l_send.at[n], l_recv.at[n], device_id=sibling, device_id_type=MESH,
        )

    for n in range(2):
        u_in[n].wait()
        mask_tiles(uown, (), umask, u_order[n])
    pl.semaphore_wait(barrier, len(partners))
    for h in range(2):
        for step in (1, 3):
            for k in range(2):
                send_u(step, k, h).start()
    u_in[3].wait()
    mask_tiles(uown, (), umask, y)
    for h in range(2):
        send_u(0, 1, h).start()
    for n in range(4):
        l_in[n].wait()
        mask_tiles(lbuf, (0,), lmask, l_order[n])
        send_l(n).start()
    u_in[2].wait()
    mask_tiles(uown, (), umask, u_order[2])
    for h in range(2):
        for k in range(2):
            send_u(2, k, h).start()
        cols = pl.ds(pl.multiple_of(core * TILE + h * COLS, COLS), COLS)
        ubuf[number(0, h), 0] = uown[rows_of(y * DEPTH, DEPTH), cols]

    def product(n, goal, q):
        rows = rows_of(goal * 2 * PIECE + q * PIECE, PIECE)
        return jnp.dot(lbuf[0, rows], ubuf[n, 0], preferred_element_type=jnp.float32) + jnp.dot(
            lbuf[1, rows], ubuf[n, 1], preferred_element_type=jnp.float32
        )

    def rows_in(n):
        return PIECE // 2 if TYPES[n] == "B" else PIECE

    def h_copy(n, q, j):
        b = SPLIT.index(n)
        sem = (b * 2 + q) * 4 + j
        return pltpu.make_async_remote_copy(
            hs.at[b, q, j], hr.at[b, q, j], h_send.at[sem], h_recv.at[sem],
            device_id=at(x, y, zb if q else za, core), device_id_type=MESH,
        )

    def x1_copy(n, q, i):
        sem = (n * 2 + q) * 2 + i
        rows = pl.ds(0, rows_in(n) + CODES)
        return pltpu.make_async_remote_copy(
            x1s.at[n, q, i, rows], x1r.at[n, q, i, rows], x1_send.at[sem], x1_recv.at[sem],
            device_id=at(xb if q else xa, y, z, core), device_id_type=MESH,
        )

    def x2_copy(n, q):
        sem = n * 2 + q
        rows = pl.ds(0, rows_in(n) + CODES)
        return pltpu.make_async_remote_copy(
            x2s.at[n, q, rows], x2r.at[n, q, rows], x2_send.at[sem], x2_recv.at[sem],
            device_id=at(xa if q else xb, y, z, core), device_id_type=MESH,
        )

    def z_copy(n, i):
        sem = n * NZ + i
        return pltpu.make_async_remote_copy(
            zs.at[n, i], zr.at[n, i], z_send.at[sem], z_recv.at[sem],
            device_id=at(x, (y + 2) % NY if UNITS[n][0] == 2 else y, (z + i) % NZ, core), device_id_type=MESH,
        )

    def y_copy(n):
        return pltpu.make_async_remote_copy(
            ys.at[n - 2], yr.at[n - 2], y_send.at[n - 2], y_recv.at[n - 2], device_id=ydev(UNITS[n][0], 0), device_id_type=MESH,
        )

    def z_steps(n):
        steps = (4, 2, 6) if TYPES[n] == "B" else (4, 3, 5, 2, 6, 1, 7)
        return steps + ((0,) if UNITS[n][0] == 2 else ())

    def arrive(n):
        s, h = UNITS[n]
        for k in (1,) if s == 0 else (0, 1):
            send_u((NY - s) % NY, k, h).wait_recv()
        if n == 0:
            for m in range(4):
                send_l(m).wait_recv()

    def multiply(n):
        arrive(n)
        if TYPES[n] == "A":
            for i in (1, 0):
                for q in range(2):
                    goal = xd if i else (xb if q else xa)
                    encode(product(n, goal, q), x1s, (n, q, i))
                    x1_copy(n, q, i).start()
            for i in (1, 0):
                for q in range(2):
                    part[n, q, i] = product(n, (xa if q else xb) if i else x, q)
        else:
            b = SPLIT.index(n)
            for j, goal in enumerate(l_order):
                for q in range(2):
                    stage[b, q, j] = product(n, goal, q)
                    encode(parity(b, q, j, 1 - odd), hs, (b, q, j))
                    h_copy(n, q, j).start()

    def parity(b, q, j, which):
        chunks = [stage[b, q, j, rows_of((which + 2 * t) * CHUNK, CHUNK)] for t in range(2)]
        return jnp.concatenate(chunks, axis=0)

    def after_h(n):
        b = SPLIT.index(n)
        half = PIECE // 2

        def summed(q, j):
            h_copy(n, q, j).wait_recv()
            return parity(b, q, j, odd) + decode(hr, (b, q, j), half)

        for q in range(2):
            encode(summed(q, 0), x1s, (n, q, 1))
            x1_copy(n, q, 1).start()
        for q in range(2):
            encode(summed(q, 2 if q else 1), x1s, (n, q, 0))
            x1_copy(n, q, 0).start()
        for q in range(2):
            part[n, q, 1, pl.ds(0, half)] = summed(q, 1 if q else 2)
            part[n, q, 0, pl.ds(0, half)] = summed(q, 3)

    def after_x1(n):
        rows = rows_in(n)
        for q in range(2):
            x1_copy(n, q, 1).wait_recv()
            encode(part[n, q, 1, pl.ds(0, rows)] + decode(x1r, (n, q, 1), rows), x2s, (n, q))
            x2_copy(n, q).start()

    def after_x2(n):
        rows = rows_in(n)
        for q in range(2):
            x1_copy(n, q, 0).wait_recv()
            x2_copy(n, q).wait_recv()
            ssum[n, pl.ds(q * rows, rows)] = (
                part[n, q, 0, pl.ds(0, rows)] + decode(x1r, (n, q, 0), rows) + decode(x2r, (n, q), rows)
            )
        for i in z_steps(n):
            encode(own_rows(n, (z + i) % NZ), zs, (n, i))
            z_copy(n, i).start()

    def own_rows(n, goal):
        spot = goal // 2 if TYPES[n] == "B" else goal
        return ssum[n, rows_of(spot * CHUNK, CHUNK)]

    def after_z(n):
        s, h = UNITS[n]
        result = None if s == 2 else own_rows(n, z)
        for i in reversed(z_steps(n)):
            z_copy(n, i).wait_recv()
            piece = decode(zr, (n, i), CHUNK)
            result = piece if result is None else result + piece
        if s in (1, 3):
            ys[n - 2] = result
            y_copy(n).start()
        else:
            total[s // 2, :, pl.ds(h * COLS, COLS)] = result

    actions = {"u": multiply, "h": after_h, "x1": after_x1, "x2": after_x2, "z": after_z}
    for action, n in ORDER:
        actions[action](n)

    for n in range(2, 6):
        y_copy(n).wait_recv()
    for h in range(2):
        cols = pl.ds(h * COLS, COLS)
        total[0, :, cols] = total[0, :, cols] + total[1, :, cols] + yr[h] + yr[2 + h]
    half = CHUNK // 2
    cs[...] = total[0, rows_of((1 - core) * half, half)]
    across = pltpu.make_async_remote_copy(cs, cr, c_send.at[0], c_recv.at[0], device_id=sibling, device_id_type=MESH)
    across.start()

    def finish(side, value):
        keep = ancestor[layer // (TILE // half), y * 2 + side].astype(jnp.float32)
        cols = pl.ds(pl.multiple_of(side * TILE, TILE), TILE)
        out[:, cols] = initial[:, cols] - keep * value

    finish(core, total[0, rows_of(core * half, half)])

    for h in range(2):
        for step in (1, 3, 2):
            for k in range(2):
                send_u(step, k, h).wait_send()
        send_u(0, 1, h).wait_send()
    for n in range(4):
        send_l(n).wait_send()
    for n in range(len(UNITS)):
        for q in range(2):
            if TYPES[n] == "B":
                for j in range(4):
                    h_copy(n, q, j).wait_send()
            x1_copy(n, q, 0).wait_send()
            x1_copy(n, q, 1).wait_send()
            x2_copy(n, q).wait_send()
        for i in z_steps(n):
            z_copy(n, i).wait_send()
        if 2 <= n < 6:
            y_copy(n).wait_send()
    across.wait_recv()
    finish(1 - core, cr[...])
    across.wait_send()


def local(l_panels, u_panels, l_masks, u_masks, ancestor_tiles, initial):
    any_spec = pl.BlockSpec(memory_space=pl.ANY)
    smem = pl.BlockSpec(memory_space=pltpu.SMEM)
    vmem = pl.BlockSpec(memory_space=pltpu.VMEM)
    dma = pltpu.SemaphoreType.DMA
    bf16, f32, i16 = jnp.bfloat16, jnp.float32, jnp.int16
    units, splits = len(UNITS), max(len(SPLIT), 1)
    halves = PIECE // 2 + CODES
    pairs = [8 * splits, 4 * units, 2 * units, NZ * units, 4, 1]
    return pl.pallas_call(
        kernel,
        out_shape=jax.ShapeDtypeStruct(initial.shape, f32),
        in_specs=[any_spec, any_spec, smem, smem, smem, vmem],
        out_specs=vmem,
        scratch_shapes=[
            pltpu.VMEM((2, 2048, DEPTH), bf16),
            pltpu.VMEM((2048, DEPTH), bf16),
            pltpu.VMEM((units, 2, DEPTH, COLS), bf16),
            pltpu.VMEM((splits, 2, 4, PIECE, COLS), f32),
            pltpu.VMEM((splits, 2, 4, halves, COLS), i16),
            pltpu.VMEM((splits, 2, 4, halves, COLS), i16),
            pltpu.VMEM((units, 2, 2, PIECE, COLS), f32),
            pltpu.VMEM((units, 2, 2, PIECE + CODES, COLS), i16),
            pltpu.VMEM((units, 2, 2, PIECE + CODES, COLS), i16),
            pltpu.VMEM((units, 2, PIECE + CODES, COLS), i16),
            pltpu.VMEM((units, 2, PIECE + CODES, COLS), i16),
            pltpu.VMEM((units, 2 * PIECE, COLS), f32),
            pltpu.VMEM((units, NZ, CHUNK + CODES, COLS), i16),
            pltpu.VMEM((units, NZ, CHUNK + CODES, COLS), i16),
            pltpu.VMEM((4, CHUNK, COLS), f32),
            pltpu.VMEM((4, CHUNK, COLS), f32),
            pltpu.VMEM((2, CHUNK, TILE), f32),
            pltpu.VMEM((CHUNK // 2, TILE), f32),
            pltpu.VMEM((CHUNK // 2, TILE), f32),
            dma((8,)),
            dma((2 * units,)), dma((2 * units,)),
            dma((4,)), dma((4,)),
            *[dma((count,)) for count in pairs for _ in range(2)],
        ],
        compiler_params=pltpu.CompilerParams(
            collective_id=0, has_side_effects=True, vmem_limit_bytes=56 * 2**20
        ),
    )(l_panels, u_panels, l_masks, u_masks, ancestor_tiles, initial)


def solution(mesh):
    return jax.shard_map(
        local,
        mesh=mesh,
        in_specs=(
            P("layer", None, "col"),
            P("layer", None, "col"),
            P("layer", None, None),
            P("layer", None, None),
            P(),
            P("layer", "col"),
        ),
        out_specs=P("layer", "col"),
        check_vma=False,
    )
```

```python
import jax
import jax.numpy as jnp
from jax import lax
from jax.experimental import pallas as pl
from jax.experimental.pallas import tpu as pltpu
from jax.sharding import PartitionSpec as P

MESH = pl.DeviceIdType.MESH
TILE = 256
NX, NY, NZ = 4, 4, 8
DEPTH = 512
PIECE = 256
CHUNK = 64
CODES = 16
COLS = 128
LEVELS = 32000.0
STEPS = 8.0


def encode(block, codes, where):
    rows, cols = block.shape
    top = jnp.maximum(jnp.max(jnp.abs(block), axis=0, keepdims=True), 2.0**-100)
    level = jnp.ceil(jnp.log2(top) * STEPS) + 1.0
    factor = jnp.exp2(level * (-1.0 / STEPS)) * LEVELS
    codes[(*where, pl.ds(0, rows), slice(None))] = jnp.round(block * factor).astype(jnp.int32).astype(jnp.int16)
    codes[(*where, pl.ds(rows, CODES), slice(None))] = (
        jnp.broadcast_to(level, (CODES, cols)).astype(jnp.int32).astype(jnp.int16)
    )


def decode(codes, where, rows):
    level = codes[(*where, pl.ds(rows, CODES), slice(None))].astype(jnp.int32).astype(jnp.float32)[0:1]
    factor = jnp.exp2(level * (1.0 / STEPS)) * (1.0 / LEVELS)
    return codes[(*where, pl.ds(0, rows), slice(None))].astype(jnp.int32).astype(jnp.float32) * factor


UNITS = ((0, 0), (0, 1), (1, 0), (1, 1), (3, 0), (3, 1), (2, 0), (2, 1))
TYPES = "ABABBABA"
ORDER = (
    ("u", 0), ("u", 1), ("x1", 0), ("u", 2), ("u", 4), ("h", 1),
    ("x2", 0), ("x1", 2), ("u", 3), ("u", 5), ("x1", 1), ("h", 4),
    ("x2", 2), ("x1", 5), ("u", 6), ("z", 0), ("x2", 1), ("h", 3),
    ("x1", 4), ("x2", 5), ("u", 7), ("x1", 3), ("z", 2), ("x2", 4),
    ("h", 6), ("x1", 7), ("x2", 3), ("z", 1), ("x1", 6), ("x2", 7),
    ("z", 5), ("x2", 6), ("z", 4), ("z", 3), ("z", 7), ("z", 6),
)
SPLIT = tuple(n for n, kind in enumerate(TYPES) if kind == "B")


def kernel(
    l_hbm, u_hbm, lmask_hbm, umask_hbm, ancestor_hbm, initial_hbm, out,
    lmask, umask, ancestor, initial,
    lbuf, uown, ubuf, stage, hs, hr, part, x1s, x1r, x2s, x2r, ssum, zs, zr, ys, yr, total, cs, cr,
    in_sem, a_send, a_recv, l_send, l_recv, h_send, h_recv, x1_send, x1_recv, x2_send, x2_recv,
    z_send, z_recv, y_send, y_recv, c_send, c_recv,
):
    layer = lax.axis_index("layer")
    y = lax.axis_index("col")
    x = layer // (2 * NZ)
    z = (layer // 2) % NZ
    core = layer % 2
    xa = x + 1 - 2 * (x % 2)
    xb = 3 - x
    xd = 3 - xa
    odd = z % 2
    za = z + 1 - 2 * odd
    zb = (z + 2 * odd + NZ - 1) % NZ

    def at(x_, y_, z_, c_):
        return ((x_ * NZ + z_) * 2 + c_, y_)

    def ydev(step, k):
        return at(x, (y + step) % NY, z, (core + k) % 2)

    sibling = at(x, y, z, 1 - core)
    partners = [sibling]
    partners += [ydev(step, k) for step in (1, 2, 3) for k in (0, 1)]
    partners += [at(xa, y, z, core), at(xb, y, z, core)]
    partners += [at(x, y, (z + i) % NZ, core) for i in range(1, NZ)]
    partners += [at(x, (y + 2) % NY, (z + i) % NZ, core) for i in range(1, NZ)]

    def rows_of(first, count):
        return pl.ds(pl.multiple_of(first, count), count)

    barrier = pltpu.get_barrier_semaphore()
    for partner in partners:
        pl.semaphore_signal(barrier, inc=1, device_id=partner, device_id_type=MESH)

    u_order = [(y + step) % NY for step in (1, 3, 2, 0)]
    l_order = [xd, xa, xb, x]
    u_in = [
        pltpu.make_async_copy(u_hbm.at[0, rows_of(b * DEPTH, DEPTH)], uown.at[rows_of(b * DEPTH, DEPTH)], in_sem.at[n])
        for n, b in enumerate(u_order)
    ]
    l_in = [
        pltpu.make_async_copy(l_hbm.at[0, rows_of(b * DEPTH, DEPTH)], lbuf.at[0, rows_of(b * DEPTH, DEPTH)], in_sem.at[4 + n])
        for n, b in enumerate(l_order)
    ]
    small = [
        pltpu.make_async_copy(source, target, in_sem.at[8 + n])
        for n, (source, target) in enumerate(
            ((umask_hbm, umask), (lmask_hbm, lmask), (ancestor_hbm, ancestor), (initial_hbm, initial))
        )
    ]
    small[0].start()
    small[1].start()
    for n in (0, 1, 3):
        u_in[n].start()
    for n in range(4):
        l_in[n].start()
    u_in[2].start()
    small[2].start()
    small[3].start()

    def mask_tiles(ref, where, mask, block):
        for t in range(2):
            rows = rows_of(block * DEPTH + t * TILE, TILE)
            for h in range(2):
                keep = mask[0, block * 2 + t, y * 2 + h].astype(jnp.float32)
                spot = (*where, rows, pl.ds(h * TILE, TILE))
                ref[spot] = ref[spot] * jnp.full((TILE, TILE), keep).astype(jnp.bfloat16)

    def number(s, h):
        return UNITS.index((s, h))

    def send_u(step, k, h):
        n = number((NY - step) % NY, h)
        cols = pl.ds(pl.multiple_of((core + k) % 2 * TILE + h * COLS, COLS), COLS)
        return pltpu.make_async_remote_copy(
            uown.at[rows_of((y + step) % NY * DEPTH, DEPTH), cols], ubuf.at[n, k],
            a_send.at[n * 2 + k], a_recv.at[n * 2 + k], device_id=ydev(step, k), device_id_type=MESH,
        )

    def send_l(n):
        rows = rows_of(l_order[n] * DEPTH, DEPTH)
        return pltpu.make_async_remote_copy(
            lbuf.at[0, rows], lbuf.at[1, rows], l_send.at[n], l_recv.at[n], device_id=sibling, device_id_type=MESH,
        )

    small[0].wait()
    for n in (0, 1, 3):
        u_in[n].wait()
        mask_tiles(uown, (), umask, u_order[n])
    small[1].wait()
    for n in range(4):
        l_in[n].wait()
        mask_tiles(lbuf, (0,), lmask, l_order[n])
    pl.semaphore_wait(barrier, len(partners))
    for h in range(2):
        for step in (1, 3):
            for k in range(2):
                send_u(step, k, h).start()
        send_u(0, 1, h).start()
        send_l(h).start()
    for n in (2, 3):
        send_l(n).start()
    for h in range(2):
        cols = pl.ds(pl.multiple_of(core * TILE + h * COLS, COLS), COLS)
        ubuf[number(0, h), 0] = uown[rows_of(y * DEPTH, DEPTH), cols]
    u_in[2].wait()
    mask_tiles(uown, (), umask, u_order[2])
    for h in range(2):
        for k in range(2):
            send_u(2, k, h).start()

    def product(n, goal, q):
        rows = rows_of(goal * 2 * PIECE + q * PIECE, PIECE)
        return jnp.dot(lbuf[0, rows], ubuf[n, 0], preferred_element_type=jnp.float32) + jnp.dot(
            lbuf[1, rows], ubuf[n, 1], preferred_element_type=jnp.float32
        )

    def rows_in(n):
        return PIECE // 2 if TYPES[n] == "B" else PIECE

    def h_copy(n, q, j):
        b = SPLIT.index(n)
        sem = (b * 2 + q) * 4 + j
        return pltpu.make_async_remote_copy(
            hs.at[b, q, j], hr.at[b, q, j], h_send.at[sem], h_recv.at[sem],
            device_id=at(x, y, zb if q else za, core), device_id_type=MESH,
        )

    def x1_copy(n, q, i):
        sem = (n * 2 + q) * 2 + i
        rows = pl.ds(0, rows_in(n) + CODES)
        return pltpu.make_async_remote_copy(
            x1s.at[n, q, i, rows], x1r.at[n, q, i, rows], x1_send.at[sem], x1_recv.at[sem],
            device_id=at(xb if q else xa, y, z, core), device_id_type=MESH,
        )

    def x2_copy(n, q):
        sem = n * 2 + q
        rows = pl.ds(0, rows_in(n) + CODES)
        return pltpu.make_async_remote_copy(
            x2s.at[n, q, rows], x2r.at[n, q, rows], x2_send.at[sem], x2_recv.at[sem],
            device_id=at(xa if q else xb, y, z, core), device_id_type=MESH,
        )

    def z_copy(n, i):
        sem = n * NZ + i
        return pltpu.make_async_remote_copy(
            zs.at[n, i], zr.at[n, i], z_send.at[sem], z_recv.at[sem],
            device_id=at(x, (y + 2) % NY if UNITS[n][0] == 2 else y, (z + i) % NZ, core), device_id_type=MESH,
        )

    def y_copy(n):
        return pltpu.make_async_remote_copy(
            ys.at[n - 2], yr.at[n - 2], y_send.at[n - 2], y_recv.at[n - 2], device_id=ydev(UNITS[n][0], 0), device_id_type=MESH,
        )

    def z_steps(n):
        steps = (4, 2, 6) if TYPES[n] == "B" else (4, 3, 5, 2, 6, 1, 7)
        return steps + ((0,) if UNITS[n][0] == 2 else ())

    def arrive(n):
        s, h = UNITS[n]
        for k in (1,) if s == 0 else (0, 1):
            send_u((NY - s) % NY, k, h).wait_recv()

    def l_ready(n, m):
        if n == ORDER[0][1] and m is not None:
            send_l(m).wait_recv()

    def multiply(n):
        arrive(n)
        if TYPES[n] == "A":
            for i in (1, 0):
                for q in range(2):
                    goal = xd if i else (xb if q else xa)
                    l_ready(n, (0, None, 1, 2)[2 * (1 - i) + q])
                    encode(product(n, goal, q), x1s, (n, q, i))
                    x1_copy(n, q, i).start()
            l_ready(n, 3)
            for i in (1, 0):
                for q in range(2):
                    part[n, q, i] = product(n, (xa if q else xb) if i else x, q)
        else:
            b = SPLIT.index(n)
            for j, goal in enumerate(l_order):
                l_ready(n, j)
                for q in range(2):
                    stage[b, q, j] = product(n, goal, q)
                    encode(parity(b, q, j, 1 - odd), hs, (b, q, j))
                    h_copy(n, q, j).start()

    def parity(b, q, j, which):
        chunks = [stage[b, q, j, rows_of((which + 2 * t) * CHUNK, CHUNK)] for t in range(2)]
        return jnp.concatenate(chunks, axis=0)

    def after_h(n):
        b = SPLIT.index(n)
        half = PIECE // 2

        def summed(q, j):
            h_copy(n, q, j).wait_recv()
            return parity(b, q, j, odd) + decode(hr, (b, q, j), half)

        for q in range(2):
            encode(summed(q, 0), x1s, (n, q, 1))
            x1_copy(n, q, 1).start()
        for q in range(2):
            encode(summed(q, 2 if q else 1), x1s, (n, q, 0))
            x1_copy(n, q, 0).start()
        for q in range(2):
            part[n, q, 1, pl.ds(0, half)] = summed(q, 1 if q else 2)
            part[n, q, 0, pl.ds(0, half)] = summed(q, 3)

    def after_x1(n):
        rows = rows_in(n)
        for q in range(2):
            x1_copy(n, q, 1).wait_recv()
            encode(part[n, q, 1, pl.ds(0, rows)] + decode(x1r, (n, q, 1), rows), x2s, (n, q))
            x2_copy(n, q).start()

    def after_x2(n):
        rows = rows_in(n)
        for q in range(2):
            x1_copy(n, q, 0).wait_recv()
            x2_copy(n, q).wait_recv()
            ssum[n, pl.ds(q * rows, rows)] = (
                part[n, q, 0, pl.ds(0, rows)] + decode(x1r, (n, q, 0), rows) + decode(x2r, (n, q), rows)
            )
        for i in z_steps(n):
            encode(own_rows(n, (z + i) % NZ), zs, (n, i))
            z_copy(n, i).start()

    def own_rows(n, goal):
        spot = goal // 2 if TYPES[n] == "B" else goal
        return ssum[n, rows_of(spot * CHUNK, CHUNK)]

    def after_z(n):
        s, h = UNITS[n]
        result = None if s == 2 else own_rows(n, z)
        for i in reversed(z_steps(n)):
            z_copy(n, i).wait_recv()
            piece = decode(zr, (n, i), CHUNK)
            result = piece if result is None else result + piece
        if s in (1, 3):
            ys[n - 2] = result
            y_copy(n).start()
        else:
            total[s // 2, :, pl.ds(h * COLS, COLS)] = result

    actions = {"u": multiply, "h": after_h, "x1": after_x1, "x2": after_x2, "z": after_z}
    for action, n in ORDER:
        actions[action](n)

    for n in range(2, 6):
        y_copy(n).wait_recv()
    for h in range(2):
        cols = pl.ds(h * COLS, COLS)
        total[0, :, cols] = total[0, :, cols] + total[1, :, cols] + yr[h] + yr[2 + h]
    half = CHUNK // 2
    cs[...] = total[0, rows_of((1 - core) * half, half)]
    across = pltpu.make_async_remote_copy(cs, cr, c_send.at[0], c_recv.at[0], device_id=sibling, device_id_type=MESH)
    across.start()

    small[2].wait()
    small[3].wait()

    def finish(side, value):
        keep = ancestor[layer // (TILE // half), y * 2 + side].astype(jnp.float32)
        cols = pl.ds(pl.multiple_of(side * TILE, TILE), TILE)
        out[:, cols] = initial[:, cols] - keep * value

    finish(core, total[0, rows_of(core * half, half)])

    for h in range(2):
        for step in (1, 3, 2):
            for k in range(2):
                send_u(step, k, h).wait_send()
        send_u(0, 1, h).wait_send()
    for n in range(4):
        send_l(n).wait_send()
    for n in range(len(UNITS)):
        for q in range(2):
            if TYPES[n] == "B":
                for j in range(4):
                    h_copy(n, q, j).wait_send()
            x1_copy(n, q, 0).wait_send()
            x1_copy(n, q, 1).wait_send()
            x2_copy(n, q).wait_send()
        for i in z_steps(n):
            z_copy(n, i).wait_send()
        if 2 <= n < 6:
            y_copy(n).wait_send()
    across.wait_recv()
    finish(1 - core, cr[...])
    across.wait_send()


def local(l_panels, u_panels, l_masks, u_masks, ancestor_tiles, initial):
    any_spec = pl.BlockSpec(memory_space=pl.ANY)
    vmem = pl.BlockSpec(memory_space=pltpu.VMEM)
    dma = pltpu.SemaphoreType.DMA
    bf16, f32, i16 = jnp.bfloat16, jnp.float32, jnp.int16
    units, splits = len(UNITS), max(len(SPLIT), 1)
    halves = PIECE // 2 + CODES
    pairs = [8 * splits, 4 * units, 2 * units, NZ * units, 4, 1]
    return pl.pallas_call(
        kernel,
        out_shape=jax.ShapeDtypeStruct(initial.shape, f32),
        in_specs=[any_spec] * 6,
        out_specs=vmem,
        scratch_shapes=[
            pltpu.SMEM(l_masks.shape, jnp.int32),
            pltpu.SMEM(u_masks.shape, jnp.int32),
            pltpu.SMEM(ancestor_tiles.shape, jnp.int32),
            pltpu.VMEM(initial.shape, f32),
            pltpu.VMEM((2, 2048, DEPTH), bf16),
            pltpu.VMEM((2048, DEPTH), bf16),
            pltpu.VMEM((units, 2, DEPTH, COLS), bf16),
            pltpu.VMEM((splits, 2, 4, PIECE, COLS), f32),
            pltpu.VMEM((splits, 2, 4, halves, COLS), i16),
            pltpu.VMEM((splits, 2, 4, halves, COLS), i16),
            pltpu.VMEM((units, 2, 2, PIECE, COLS), f32),
            pltpu.VMEM((units, 2, 2, PIECE + CODES, COLS), i16),
            pltpu.VMEM((units, 2, 2, PIECE + CODES, COLS), i16),
            pltpu.VMEM((units, 2, PIECE + CODES, COLS), i16),
            pltpu.VMEM((units, 2, PIECE + CODES, COLS), i16),
            pltpu.VMEM((units, 2 * PIECE, COLS), f32),
            pltpu.VMEM((units, NZ, CHUNK + CODES, COLS), i16),
            pltpu.VMEM((units, NZ, CHUNK + CODES, COLS), i16),
            pltpu.VMEM((4, CHUNK, COLS), f32),
            pltpu.VMEM((4, CHUNK, COLS), f32),
            pltpu.VMEM((2, CHUNK, TILE), f32),
            pltpu.VMEM((CHUNK // 2, TILE), f32),
            pltpu.VMEM((CHUNK // 2, TILE), f32),
            dma((12,)),
            dma((2 * units,)), dma((2 * units,)),
            dma((4,)), dma((4,)),
            *[dma((count,)) for count in pairs for _ in range(2)],
        ],
        compiler_params=pltpu.CompilerParams(
            collective_id=0, has_side_effects=True, vmem_limit_bytes=56 * 2**20
        ),
    )(l_panels, u_panels, l_masks, u_masks, ancestor_tiles, initial)


def solution(mesh):
    return jax.shard_map(
        local,
        mesh=mesh,
        in_specs=(
            P("layer", None, "col"),
            P("layer", None, "col"),
            P("layer", None, None),
            P("layer", None, None),
            P(),
            P("layer", "col"),
        ),
        out_specs=P("layer", "col"),
        check_vma=False,
    )
```
